512 devices in a mesh: dp: 32 (over y, z_lo), tensor: 16 (over z_hi, x, core).
Axes of the slice: x: 4, y: 4, z: 16 (z_hi: 2, z_lo: 8; z = z_hi * 8 + z_lo), core: 2. Of those that a mesh axis runs over, the one named last changes fastest.
Arguments:
- tokens: bfloat16 [32768, 4608], P(('dp', 'tensor')), may hold values from -24 to 24
- gain: float32 [4608], replicated, may hold values from 0.1 to 1.9
- qk_weight: bfloat16 [4608, 2, 2048], P('dp', None, 'tensor'), may hold values from -0.54506148 to 0.54506148
- value_rows: bfloat16 [32768, 2048], P(('dp', 'tensor')), may hold values from -6 to 6
- context_grad: bfloat16 [32768, 2048], P(('dp', 'tensor')), may hold values from -6 to 6
- first_key: int32 [32768], P('dp'), may hold values from 0 to 32767, as said below
Outputs:
- qkv_grad: bfloat16 [4608, 3, 2048], P('dp', None, 'tensor')
The draws below stay inside these ranges and needn't reach their ends.
Inputs may be any that keep to these rules, and one draw needn't show every extreme that they name: first_key[i] is the larger of the first position of token i's document and i - 4095; documents stay inside their sequence of 1024 tokens, the last token of each sequence is a document of its own, and first_key[i] <= i.
All inputs are finite; a program needn't handle non-finite values.
Results may differ from the reference program's by a relative error of at most 0.03.
The reference program's roundings to bfloat16 on the way count: a program that leaves them out, or rounds other values in their place, can miss the bound.
Values may be sent and summed in bfloat16 or wider, within the bound.
A program may use at most 64 MiB of HBM per device.

```python
import jax
import jax.numpy as jnp
from jax import lax

D = 4608
HD = 128
WINDOW = 4096
HEADS = 16
SEQ = 1024
TOKENS = 32768
N_DP = 32


def draw_first_key(key, part):
    key = jax.random.fold_in(key, 11)
    marks = jax.random.randint(key, (N_DP, SEQ), 0, 40) == 0
    places = jnp.arange(SEQ, dtype=jnp.int32)
    marks = marks | (places[None, :] == 0) | (places[None, :] == SEQ - 1)
    starts = lax.cummax(jnp.where(marks, places[None, :], 0), axis=1)
    starts = jnp.maximum(starts, places[None, :] - WINDOW + 1)
    base = (jnp.arange(N_DP, dtype=jnp.int32) * SEQ)[:, None]
    return (starts + base).reshape(TOKENS).astype(jnp.int32)


def draw_qk_weight(key, part):
    key = jax.random.fold_in(key, 23)
    scale_key, entry_key = jax.random.split(key)
    head_rank = jax.random.permutation(scale_key, HEADS).astype(jnp.float32)
    factors = 8.0 ** (head_rank / max(HEADS - 1, 1))
    column_factor = jnp.repeat(factors, HD)
    entries = jnp.clip(jax.random.normal(entry_key, (D, 2, HEADS * HD), jnp.float32), -4.5, 4.5)
    return (entries * column_factor[None, None, :] * D ** (-0.5)).astype(jnp.bfloat16)


def with_spikes(values, stream_key, source, target, parts, factor):
    owner, partner = [(jnp.arange(values.shape[position]) // (values.shape[position] // parts)).reshape([-1 if axis == position else 1 for axis in range(values.ndim)]) for position in (source, target)]
    chosen = jax.random.permutation(stream_key, parts)[partner]
    strong = (owner == chosen) | (owner == (partner + parts // 2) % parts)
    return jnp.where(strong, factor * values, values)


def level_of(stream_key, dims, cuts, low, top_value):
    def one(axis_at, parts):
        steps = jax.random.uniform(jax.random.fold_in(jax.random.fold_in(stream_key, 6), axis_at), (parts,), jnp.float32, low / len(cuts), top_value / len(cuts))
        return jnp.repeat(jnp.exp(steps), dims[axis_at] // parts).reshape((-1,) + (1,) * (len(dims) - axis_at - 1))

    factor_of = one(*cuts[0])
    for cut in cuts[1:]:
        factor_of = factor_of * one(*cut)
    return factor_of


def noise(key, dims, scale, limit, shards=(), kind=jnp.bfloat16):
    loudness = level_of(key, dims, shards, -0.22, 0.18) if shards else 1.0
    array = jax.random.normal(key, dims, jnp.float32) * scale * loudness
    return jnp.minimum(jnp.maximum(array, -limit), limit).astype(kind)


def gaussian_with(own_key, extent, deviation, bound, cuts, heavy, kind=jnp.bfloat16):
    array = deviation * jax.random.normal(own_key, extent, jnp.float32)
    if cuts:
        array = array * level_of(own_key, extent, cuts, -0.22, 0.18)
    return jnp.clip(with_spikes(array, jax.random.fold_in(own_key, 3), *heavy), -bound, bound).astype(kind)


def setup_inputs(seed: int = 0) -> dict:
    key_list = jax.random.split(jax.random.key(seed), 7)
    tokens = gaussian_with(key_list[0], (TOKENS, D), 1.0, 24.0, ((0, 512),), (0, 1, 512, 6.0))
    gain = jnp.clip(1.0 + 0.18 * jax.random.normal(key_list[1], (D,), jnp.float32), 0.1, 1.9)
    qk_weight = draw_qk_weight(jax.random.fold_in(key_list[6], 71), 0)
    value_rows = noise(key_list[3], (TOKENS, HEADS * HD), 1.0, 6.0, ((0, 512),))
    context_grad = noise(key_list[4], (TOKENS, HEADS * HD), 1.0, 6.0, ((0, 512),))
    first_key = draw_first_key(jax.random.fold_in(key_list[6], 71), 0)
    return {"tokens": tokens, "gain": gain, "qk_weight": qk_weight, "value_rows": value_rows, "context_grad": context_grad, "first_key": first_key}


epsilon = 1e-06
softcap = 50.0
query_scale = 144.0 ** (-0.5)

def reference(tokens, gain, qk_weight, value_rows, context_grad, first_key):
    head_cols = HEADS * HD
    whole_w = qk_weight.reshape(D, 2 * head_cols)

    def replica(total, replica_index):
        offset = (replica_index * SEQ).astype(jnp.int32)
        row_block = lax.dynamic_slice_in_dim(tokens, offset, SEQ, 0)
        grad_block = lax.dynamic_slice_in_dim(context_grad, offset, SEQ, 0)
        value_block = lax.dynamic_slice_in_dim(value_rows, offset, SEQ, 0)
        starts = lax.dynamic_slice_in_dim(first_key, offset, SEQ, 0)
        floated = row_block.astype(jnp.float32)
        mean_sq = lax.optimization_barrier(jnp.mean(floated * floated, axis=1, keepdims=True))
        normed = (floated * lax.rsqrt(mean_sq + epsilon) * gain.astype(jnp.float32)).astype(jnp.bfloat16)
        projected = jnp.dot(normed, whole_w, preferred_element_type=jnp.float32).astype(jnp.bfloat16)
        projected = projected.reshape(SEQ, 2, HEADS, HD).astype(jnp.float32)
        queries = projected[:, 0]
        keys_all = projected[:, 1]
        values_all = value_block.reshape(SEQ, HEADS, HD).astype(jnp.float32)
        raw = jnp.einsum('qhd,khd->hqk', queries, keys_all) * query_scale
        tanh_val = jnp.tanh(raw / softcap)
        capped = softcap * tanh_val
        positions = offset + jnp.arange(SEQ, dtype=jnp.int32)
        seen = (positions[None, :] >= starts[:, None]) & (positions[None, :] <= positions[:, None])
        raised = jnp.where(seen[None], jnp.exp(capped), 0.0)
        probs = raised / lax.optimization_barrier(jnp.sum(raised, axis=2, keepdims=True))
        probs_low = probs.astype(jnp.bfloat16).astype(jnp.float32)
        cotangent = grad_block.reshape(SEQ, HEADS, HD).astype(jnp.float32)
        value_grad = jnp.einsum('hqk,qhd->khd', probs_low, cotangent).astype(jnp.bfloat16)
        dprobs = jnp.einsum('qhd,khd->hqk', cotangent, values_all)
        inner = lax.optimization_barrier(jnp.sum(probs * dprobs, axis=2, keepdims=True))
        dscore = (probs * (dprobs - inner) * (1.0 - tanh_val * tanh_val) * query_scale).astype(jnp.bfloat16).astype(jnp.float32)
        query_grad = jnp.einsum('hqk,khd->qhd', dscore, keys_all).astype(jnp.bfloat16)
        key_grad = jnp.einsum('hqk,qhd->khd', dscore, queries).astype(jnp.bfloat16)
        stacked = jnp.stack([query_grad, key_grad, value_grad], axis=1).reshape(SEQ, 3 * head_cols)
        partial_sum = lax.dot_general(normed, stacked, (((0,), (0,)), ((), ())), preferred_element_type=jnp.float32)
        partial_low = lax.optimization_barrier(partial_sum.astype(jnp.bfloat16))
        return (total + partial_low.astype(jnp.float32), None)
    start_total = jnp.zeros((D, 3 * head_cols), jnp.float32)
    total, unused = lax.scan(replica, start_total, jnp.arange(N_DP, dtype=jnp.int32))
    return total.astype(jnp.bfloat16).reshape(D, 3, head_cols)
```

```python
import functools

import jax
import jax.numpy as jnp
from jax import lax
from jax.experimental import pallas as pl
from jax.experimental.pallas import tpu as pltpu
from jax.sharding import PartitionSpec as P

MESH = pl.DeviceIdType.MESH
HD = 128
epsilon = 1e-06
softcap = 50.0
query_scale = 144.0 ** (-0.5)
NX, NY, NL = 4, 4, 8
SEQ = 1024
D = 4608
BLK = 144
QR = 16
NQ = 4
VMEM = pl.BlockSpec(memory_space=pltpu.VMEM)


def where_am_i():
    dp, t = lax.axis_index("dp"), lax.axis_index("tensor")
    return dp // NL, dp % NL, t // 8, (t // 2) % NX, t % 2


def device(y, zl, zh, x, c):
    return (y * NL + zl, zh * 8 + x * 2 + c)


def signal(target):
    pl.semaphore_signal(
        pltpu.get_barrier_semaphore(), inc=1, device_id=target, device_id_type=MESH
    )


class Sems:
    def __init__(self):
        self.at = {}
        self.n = 0

    def block(self, name, count):
        self.at[name] = self.n
        self.n += count


K1 = Sems()
for name, count in (
    ("L", 8), ("R", 8), ("O", 8), ("C", 32), ("Z", 4),
    ("WR", 8), ("WL", 8), ("YL", 8), ("YR", 8), ("YO", 8), ("AC", 16), ("AV", 16),
):
    K1.block(name, count)


def gather_kernel(
    tok, gain, w, ctx, val, nrm, proj, ctxo, valo, w_all, ssem, rsem
):
    y, zl, zh, x, c = where_am_i()
    me = zh * 8 + x * 2 + c
    left, right = (x + NX - 1) % NX, (x + 1) % NX
    opp = (x + 2) % NX
    to_left, to_right = device(y, zl, zh, left, c), device(y, zl, zh, right, c)
    to_core = device(y, zl, zh, x, 1 - c)
    to_far = device(y, zl, 1 - zh, x, c)
    y_lo, y_hi, y_op = (y + NY - 1) % NY, (y + 1) % NY, (y + 2) % NY
    to_ylo, to_yhi = device(y_lo, zl, zh, x, c), device(y_hi, zl, zh, x, c)
    has_lo, has_hi = zl > 0, zl < NL - 1
    to_zlo, to_zhi = device(y, zl - 1, zh, x, c), device(y, zl + 1, zh, x, c)

    def peer(d):
        t = (me + d) % 16
        return (y * NL + zl, t)

    for d in range(1, 16):
        signal(peer(d))
    signal(to_ylo)
    signal(to_yhi)

    @pl.when(has_lo)
    def _():
        signal(to_zlo)

    @pl.when(has_hi)
    def _():
        signal(to_zhi)

    own = me * 64
    for q in range(NQ):
        t = tok[q * QR : (q + 1) * QR, :].astype(jnp.float32)
        mean_sq = jnp.mean(t * t, axis=1, keepdims=True)
        n = (t * lax.rsqrt(mean_sq + epsilon) * gain[...]).astype(jnp.bfloat16)
        nrm[pl.ds(pl.multiple_of(own + q * QR, QR), QR), :] = n
    w_all[pl.ds(pl.multiple_of((y * NL + zl) * BLK, 16), BLK), :] = w[...]

    ends = (zl == 0).astype(jnp.int32) + (zl == NL - 1).astype(jnp.int32)
    pl.semaphore_wait(pltpu.get_barrier_semaphore(), 19 - ends)

    sent = []
    used = [0]

    def send(src, dst, r, target, cond=None):
        s = used[0]
        used[0] += 1
        copy = pltpu.make_async_remote_copy(
            src_ref=src, dst_ref=dst, send_sem=ssem.at[s], recv_sem=rsem.at[r],
            device_id=target, device_id_type=MESH,
        )
        copy.start()
        sent.append(copy)

    def got(ref, r):
        pltpu.make_async_remote_copy(
            src_ref=ref, dst_ref=ref, send_sem=ssem.at[0], recv_sem=rsem.at[r],
            device_id=to_core, device_id_type=MESH,
        ).wait_recv()

    def rows(h, xx, cc, q):
        r = h * 512 + xx * 128 + cc * 64 + q * QR
        return nrm.at[pl.ds(pl.multiple_of(r, QR), QR), :]

    def wrows(yy, b):
        return w_all.at[pl.ds(pl.multiple_of((yy * NL + b) * BLK, 16), BLK), :]

    def to_sister(k, h, xx, q):
        send(rows(h, xx, c, q), rows(h, xx, c, q), K1.at["C"] + k * 16 + xx * 4 + q, to_core)

    def spread(k, h, q):
        mine = rows(h, x, c, q)
        send(mine, mine, K1.at["L"] + k * 4 + q, to_right)
        send(mine, mine, K1.at["R"] + k * 4 + q, to_left)
        to_sister(k, h, x, q)

    def relay(k, h, q):
        from_left, from_right = rows(h, left, c, q), rows(h, right, c, q)
        got(from_left, K1.at["L"] + k * 4 + q)
        if q % 2 == 0:
            send(from_left, from_left, K1.at["O"] + k * 4 + q, to_right)
        to_sister(k, h, left, q)
        got(from_right, K1.at["R"] + k * 4 + q)
        if q % 2 == 1:
            send(from_right, from_right, K1.at["O"] + k * 4 + q, to_left)
        to_sister(k, h, right, q)

    def last(k, h, q):
        got(rows(h, opp, c, q), K1.at["O"] + k * 4 + q)
        to_sister(k, h, opp, q)

    far = 1 - zh
    for q in range(NQ):
        send(rows(zh, x, c, q), rows(zh, x, c, q), K1.at["Z"] + q, to_far)

    line = []
    s_line = used[0]
    used[0] += 16

    def along(cond, src, s, r, target):
        def copy():
            return pltpu.make_async_remote_copy(
                src_ref=src, dst_ref=src, send_sem=ssem.at[s_line + s],
                recv_sem=rsem.at[r], device_id=target, device_id_type=MESH,
            )

        @pl.when(cond)
        def _():
            copy().start()

        line.append((cond, copy))

    along(has_hi, wrows(y, zl), 0, K1.at["WR"] + 1, to_zhi)
    along(has_lo, wrows(y, zl), 8, K1.at["WL"] + 1, to_zlo)

    for q in range(NQ):
        spread(0, zh, q)

    s_y = used[0]
    used[0] += 16

    def y_copies(b):
        ref = wrows(y, b)
        return (
            pltpu.make_async_remote_copy(
                src_ref=ref, dst_ref=ref, send_sem=ssem.at[s_y + b],
                recv_sem=rsem.at[K1.at["YL"] + b], device_id=to_yhi, device_id_type=MESH,
            ),
            pltpu.make_async_remote_copy(
                src_ref=ref, dst_ref=ref, send_sem=ssem.at[s_y + 8 + b],
                recv_sem=rsem.at[K1.at["YR"] + b], device_id=to_ylo, device_id_type=MESH,
            ),
        )

    def y_spread(b):
        for copy in y_copies(b):
            copy.start()

    y_spread(zl)

    for d in range(1, 16):
        t = (me + d) % 16
        cols = pl.ds(pl.multiple_of(t * HD, HD), HD)
        here = pl.ds(pl.multiple_of(me * 64, 64), 64)
        send(ctx.at[:, cols], ctxo.at[here, :], K1.at["AC"] + d, peer(d))
        send(val.at[:, cols], valo.at[here, :], K1.at["AV"] + d, peer(d))
    here = pl.ds(pl.multiple_of(me * 64, 64), 64)
    mycols = pl.ds(pl.multiple_of(me * HD, HD), HD)
    ctxo[here, :] = ctx[:, mycols]
    valo[here, :] = val[:, mycols]

    def line_step(t):
        lo_ok, hi_ok = zl - t >= 0, zl + t <= NL - 1
        b_lo, b_hi = jnp.maximum(zl - t, 0), jnp.minimum(zl + t, NL - 1)

        @pl.when(lo_ok)
        def _():
            got(wrows(y, b_lo), K1.at["WR"] + t)

        if t < NL - 1:
            along(lo_ok & has_hi, wrows(y, b_lo), t, K1.at["WR"] + t + 1, to_zhi)

        @pl.when(lo_ok)
        def _():
            y_spread(b_lo)

        @pl.when(hi_ok)
        def _():
            got(wrows(y, b_hi), K1.at["WL"] + t)

        if t < NL - 1:
            along(hi_ok & has_lo, wrows(y, b_hi), 8 + t, K1.at["WL"] + t + 1, to_zlo)

        @pl.when(hi_ok)
        def _():
            y_spread(b_hi)

    line_step(1)
    relay(0, zh, 0)
    line_step(2)
    relay(0, zh, 1)
    last(0, zh, 0)
    line_step(3)
    relay(0, zh, 2)
    last(0, zh, 1)
    line_step(4)
    relay(0, zh, 3)
    last(0, zh, 2)
    line_step(5)
    last(0, zh, 3)
    line_step(6)
    line_step(7)
    for b in range(NL):
        lo, hi = wrows(y_lo, b), wrows(y_hi, b)
        got(lo, K1.at["YL"] + b)
        if b % 2 == 0:
            send(lo, lo, K1.at["YO"] + b, to_yhi)
        got(hi, K1.at["YR"] + b)
        if b % 2 == 1:
            send(hi, hi, K1.at["YO"] + b, to_ylo)
    for b in range(NL):
        got(wrows(y_op, b), K1.at["YO"] + b)

    def sister(k, h):
        for xx in range(NX):
            for q in range(NQ):
                got(rows(h, xx, 1 - c, q), K1.at["C"] + k * 16 + xx * 4 + q)

    def project(h):
        for r in range(2):
            part = pl.ds(pl.multiple_of(h * 512 + r * 256, 256), 256)
            proj[part, :] = jnp.dot(
                nrm[part, :], w_all[...], preferred_element_type=jnp.float32
            ).astype(jnp.bfloat16)

    sister(0, zh)
    project(zh)
    for q in range(NQ):
        got(rows(far, x, c, q), K1.at["Z"] + q)
        spread(1, far, q)
        if q > 0:
            relay(1, far, q - 1)
        if q > 1:
            last(1, far, q - 2)
    relay(1, far, NQ - 1)
    last(1, far, NQ - 2)
    last(1, far, NQ - 1)
    sister(1, far)
    project(far)
    for d in range(1, 16):
        t = (me + 16 - d) % 16
        there = pl.ds(pl.multiple_of(t * 64, 64), 64)
        got(ctxo.at[there, :], K1.at["AC"] + d)
        got(valo.at[there, :], K1.at["AV"] + d)
    for copy in sent:
        copy.wait_send()
    for cond, copy in line:

        @pl.when(cond)
        def _(copy=copy):
            copy().wait_send()

    for b in range(NL):
        for copy in y_copies(b):
            copy.wait_send()


N_SEND1 = 4 + 16 + 16 + 12 + 12 + 30 + 2 * (8 + 4 + 4) + 8 + 16


def attention_kernel(proj, ctx, val, start, out, dk_acc, dv_acc):
    qb = 256
    f32 = jnp.float32
    dk_acc[...] = jnp.zeros_like(dk_acc)
    dv_acc[...] = jnp.zeros_like(dv_acc)
    nt = (((1,), (1,)), ((), ()))
    tn = (((0,), (0,)), ((), ()))
    for i in range(SEQ // qb):
        lo, nk = i * qb, (i + 1) * qb
        q = proj[lo:nk, 0:HD]
        k = proj[0:nk, HD : 2 * HD]
        cot = ctx[lo:nk, :]
        raw = lax.dot_general(q, k, nt, preferred_element_type=f32)
        t = jnp.tanh(raw * (query_scale / softcap))
        keys = lax.broadcasted_iota(jnp.int32, (qb, nk), 1)
        pos = lo + lax.broadcasted_iota(jnp.int32, (qb, nk), 0)
        seen = (keys >= start[lo:nk, :]) & (keys <= pos)
        raised = jnp.where(seen, jnp.exp(t * softcap), 0.0)
        probs = raised * (1.0 / jnp.sum(raised, axis=1, keepdims=True))
        low = probs.astype(jnp.bfloat16)
        dv_acc[0:nk, :] += lax.dot_general(low, cot, tn, preferred_element_type=f32)
        dprobs = lax.dot_general(cot, val[0:nk, :], nt, preferred_element_type=f32)
        inner = jnp.sum(probs * dprobs, axis=1, keepdims=True)
        ds = (probs * (dprobs - inner) * ((1.0 - t * t) * query_scale)).astype(jnp.bfloat16)
        out[lo:nk, 0:HD] = jnp.dot(ds, k, preferred_element_type=f32).astype(jnp.bfloat16)
        dk_acc[0:nk, :] += lax.dot_general(ds, q, tn, preferred_element_type=f32)
    out[:, HD : 2 * HD] = dk_acc[...].astype(jnp.bfloat16)
    out[:, 2 * HD :] = dv_acc[...].astype(jnp.bfloat16)


K3 = Sems()
for name, count in (
    ("FL", 8), ("FR", 8), ("OL", 8), ("OR", 8), ("ZR", 8), ("ZL", 8),
):
    K3.block(name, count)
ORDER = (7, 0, 6, 1, 5, 2, 4, 3)


def scatter_kernel(
    nrm, grads, out, part, f_l, f_r, o_l, o_r, z_r, z_l, stage, total, ssem, rsem
):
    y, zl, zh, x, c = where_am_i()
    y_lo, y_hi, y_op = (y + NY - 1) % NY, (y + 1) % NY, (y + 2) % NY
    to_ylo, to_yhi = device(y_lo, zl, zh, x, c), device(y_hi, zl, zh, x, c)
    has_lo, has_hi = zl > 0, zl < NL - 1
    to_zlo, to_zhi = device(y, zl - 1, zh, x, c), device(y, zl + 1, zh, x, c)
    signal(to_ylo)
    signal(to_yhi)

    @pl.when(has_lo)
    def _():
        signal(to_zlo)

    @pl.when(has_hi)
    def _():
        signal(to_zhi)

    f32, bf16 = jnp.float32, jnp.bfloat16
    wide = D // NY

    def compute(slot, yy):
        cols = pl.ds(pl.multiple_of(yy * wide, 128), wide)
        part[slot] = lax.dot_general(
            nrm[:, cols], grads[...], (((0,), (0,)), ((), ())), preferred_element_type=f32
        ).astype(bf16)

    compute(2, y_op)
    ends = (zl == 0).astype(jnp.int32) + (zl == NL - 1).astype(jnp.int32)
    pl.semaphore_wait(pltpu.get_barrier_semaphore(), 4 - ends)

    sent = []
    used = [0]

    def send(src, dst, r, target):
        s = used[0]
        used[0] += 1
        copy = pltpu.make_async_remote_copy(
            src_ref=src, dst_ref=dst, send_sem=ssem.at[s], recv_sem=rsem.at[r],
            device_id=target, device_id_type=MESH,
        )
        copy.start()
        sent.append(copy)

    def got(ref, r):
        pltpu.make_async_remote_copy(
            src_ref=ref, dst_ref=ref, send_sem=ssem.at[0], recv_sem=rsem.at[r],
            device_id=to_yhi, device_id_type=MESH,
        ).wait_recv()

    def rows(b):
        return slice(b * BLK, (b + 1) * BLK)

    for i, b in enumerate(ORDER):
        src = part.at[2, rows(b), :]
        if i % 2 == 0:
            send(src, f_l.at[rows(b), :], K3.at["FL"] + b, to_yhi)
        else:
            send(src, f_r.at[rows(b), :], K3.at["FR"] + b, to_ylo)
    compute(1, y_hi)
    compute(3, y_lo)
    for i, b in enumerate(ORDER):
        if i % 2 == 0:
            got(f_l.at[rows(b), :], K3.at["FL"] + b)
            part[1, rows(b), :] = (
                part[1, rows(b), :].astype(f32) + f_l[rows(b), :].astype(f32)
            ).astype(bf16)
        else:
            got(f_r.at[rows(b), :], K3.at["FR"] + b)
            part[3, rows(b), :] = (
                part[3, rows(b), :].astype(f32) + f_r[rows(b), :].astype(f32)
            ).astype(bf16)
        send(part.at[1, rows(b), :], o_l.at[rows(b), :], K3.at["OL"] + b, to_yhi)
        send(part.at[3, rows(b), :], o_r.at[rows(b), :], K3.at["OR"] + b, to_ylo)
    compute(0, y)
    for b in ORDER:
        got(o_l.at[rows(b), :], K3.at["OL"] + b)
        got(o_r.at[rows(b), :], K3.at["OR"] + b)
        total[rows(b), :] = (
            part[0, rows(b), :].astype(f32)
            + o_l[rows(b), :].astype(f32)
            + o_r[rows(b), :].astype(f32)
        )

    line = []
    s_line = used[0]
    used[0] += 16

    def at(b):
        return pl.ds(pl.multiple_of(b * BLK, 16), BLK)

    def pass_on(s, cond, b, first, inbox, box_name, stage, target, slot):
        def copy():
            return pltpu.make_async_remote_copy(
                src_ref=stage.at[at(b), :], dst_ref=inbox.at[at(b), :],
                send_sem=ssem.at[s_line + slot], recv_sem=rsem.at[K3.at[box_name] + b],
                device_id=target, device_id_type=MESH,
            )

        @pl.when(cond)
        def _():
            @pl.when(jnp.logical_not(first))
            def _():
                got(inbox.at[at(b), :], K3.at[box_name] + b)
                stage[at(b), :] = (
                    total[at(b), :] + inbox[at(b), :].astype(f32)
                ).astype(bf16)

            @pl.when(first)
            def _():
                stage[at(b), :] = total[at(b), :].astype(bf16)

            copy().start()

        line.append((cond, copy))

    for s in range(NL - 1):
        b = jnp.minimum(NL - 1 + zl - s, NL - 1)
        pass_on(s, s >= zl, b, zl == 0, z_r, "ZR", stage, to_zhi, s)
        b = jnp.maximum(s - (NL - 1) + zl, 0)
        pass_on(s, s >= NL - 1 - zl, b, zl == NL - 1, z_l, "ZL", stage, to_zlo, 8 + s)

    @pl.when(has_lo)
    def _():
        got(z_r.at[at(zl), :], K3.at["ZR"] + zl)
        total[at(zl), :] += z_r[at(zl), :].astype(f32)

    @pl.when(has_hi)
    def _():
        got(z_l.at[at(zl), :], K3.at["ZL"] + zl)
        total[at(zl), :] += z_l[at(zl), :].astype(f32)

    out[...] = total[at(zl), :].astype(bf16)
    for copy in sent:
        copy.wait_send()
    for cond, copy in line:

        @pl.when(cond)
        def _(copy=copy):
            copy().wait_send()


N_SEND3 = 8 + 16 + 16


def local(tokens, gain, qk_weight, value_rows, context_grad, first_key):
    sds = jax.ShapeDtypeStruct
    bf16 = jnp.bfloat16
    w = qk_weight.reshape(BLK, 2 * HD)
    nrm, proj, ctx, val = pl.pallas_call(
        gather_kernel,
        out_shape=(
            sds((SEQ, D), bf16), sds((SEQ, 2 * HD), bf16),
            sds((SEQ, HD), bf16), sds((SEQ, HD), bf16),
        ),
        in_specs=[VMEM] * 5,
        out_specs=(VMEM,) * 4,
        scratch_shapes=[
            pltpu.VMEM((D, 2 * HD), bf16),
            pltpu.SemaphoreType.DMA((N_SEND1,)),
            pltpu.SemaphoreType.DMA((K1.n,)),
        ],
        compiler_params=pltpu.CompilerParams(
            collective_id=0, has_side_effects=True, vmem_limit_bytes=56 << 20
        ),
        name="gather",
    )(tokens, gain.reshape(1, D), w, context_grad, value_rows)
    start = (first_key - lax.axis_index("dp") * SEQ).reshape(SEQ, 1)
    grads = pl.pallas_call(
        attention_kernel,
        out_shape=sds((SEQ, 3 * HD), bf16),
        in_specs=[VMEM] * 4,
        out_specs=VMEM,
        scratch_shapes=[pltpu.VMEM((SEQ, HD), jnp.float32)] * 2,
        compiler_params=pltpu.CompilerParams(vmem_limit_bytes=56 << 20),
        name="attention",
    )(proj, ctx, val, start)
    wide = D // NY
    half = pltpu.VMEM((wide, 3 * HD), bf16)
    out = pl.pallas_call(
        scatter_kernel,
        out_shape=sds((BLK, 3 * HD), bf16),
        in_specs=[VMEM] * 2,
        out_specs=VMEM,
        scratch_shapes=[
            pltpu.VMEM((4, wide, 3 * HD), bf16),
            half, half, half, half, half, half, half,
            pltpu.VMEM((wide, 3 * HD), jnp.float32),
            pltpu.SemaphoreType.DMA((N_SEND3,)),
            pltpu.SemaphoreType.DMA((K3.n,)),
        ],
        compiler_params=pltpu.CompilerParams(
            collective_id=1, has_side_effects=True, vmem_limit_bytes=56 << 20
        ),
        name="scatter",
    )(nrm, grads)
    return out.reshape(BLK, 3, HD)


def solution(mesh):
    placed = (
        P(("dp", "tensor"), None),
        P(),
        P("dp", None, "tensor"),
        P(("dp", "tensor"), None),
        P(("dp", "tensor"), None),
        P("dp"),
    )
    return jax.shard_map(
        local, mesh=mesh, in_specs=placed, out_specs=P("dp", None, "tensor"), check_vma=False
    )
```

```python
import functools

import jax
import jax.numpy as jnp
from jax import lax
from jax.experimental import pallas as pl
from jax.experimental.pallas import tpu as pltpu
from jax.sharding import PartitionSpec as P

MESH = pl.DeviceIdType.MESH
HD = 128
epsilon = 1e-06
softcap = 50.0
query_scale = 144.0 ** (-0.5)
NX, NY, NL = 4, 4, 8
SEQ = 1024
D = 4608
BLK = 144
QR = 16
NQ = 4
VMEM = pl.BlockSpec(memory_space=pltpu.VMEM)


def where_am_i():
    dp, t = lax.axis_index("dp"), lax.axis_index("tensor")
    return dp // NL, dp % NL, t // 8, (t // 2) % NX, t % 2


def device(y, zl, zh, x, c):
    return (y * NL + zl, zh * 8 + x * 2 + c)


def signal(target):
    pl.semaphore_signal(
        pltpu.get_barrier_semaphore(), inc=1, device_id=target, device_id_type=MESH
    )


class Sems:
    def __init__(self):
        self.at = {}
        self.n = 0

    def block(self, name, count):
        self.at[name] = self.n
        self.n += count


SEM = Sems()
for name, count in (
    ("L", 8), ("R", 8), ("O", 8), ("C", 32), ("Z", 4), ("WR", 8), ("WL", 8),
    ("YL", 8), ("YR", 8), ("YO", 8), ("AC", 16), ("AV", 16),
    ("FL", 8), ("FR", 8), ("OL", 8), ("OR", 8), ("ZR", 8), ("ZL", 8),
):
    SEM.block(name, count)
N_SEND = 240
WIDE = D // NY


def attention(proj, ctx, val, start, out, dk_acc, dv_acc):
    qb = 256
    f32 = jnp.float32
    dk_acc[...] = jnp.zeros_like(dk_acc)
    dv_acc[...] = jnp.zeros_like(dv_acc)
    nt = (((1,), (1,)), ((), ()))
    tn = (((0,), (0,)), ((), ()))
    for i in range(SEQ // qb):
        lo, nk = i * qb, (i + 1) * qb
        q = proj[lo:nk, 0:HD]
        k = proj[0:nk, HD : 2 * HD]
        cot = ctx[lo:nk, :]
        raw = lax.dot_general(q, k, nt, preferred_element_type=f32)
        t = jnp.tanh(raw * (query_scale / softcap))
        keys = lax.broadcasted_iota(jnp.int32, (qb, nk), 1)
        pos = lo + lax.broadcasted_iota(jnp.int32, (qb, nk), 0)
        seen = (keys >= start[lo:nk, :]) & (keys <= pos)
        raised = jnp.where(seen, jnp.exp(t * softcap), 0.0)
        probs = raised * (1.0 / jnp.sum(raised, axis=1, keepdims=True))
        low = probs.astype(jnp.bfloat16)
        dv_acc[0:nk, :] += lax.dot_general(low, cot, tn, preferred_element_type=f32)
        dprobs = lax.dot_general(cot, val[0:nk, :], nt, preferred_element_type=f32)
        inner = jnp.sum(probs * dprobs, axis=1, keepdims=True)
        ds = (probs * (dprobs - inner) * ((1.0 - t * t) * query_scale)).astype(jnp.bfloat16)
        out[lo:nk, 0:HD] = jnp.dot(ds, k, preferred_element_type=f32).astype(jnp.bfloat16)
        dk_acc[0:nk, :] += lax.dot_general(ds, q, tn, preferred_element_type=f32)
    out[:, HD : 2 * HD] = dk_acc[...].astype(jnp.bfloat16)
    out[:, 2 * HD :] = dv_acc[...].astype(jnp.bfloat16)


def kernel(
    tok, gain, w, ctx, val, start, out,
    nrm, grads_t, w_all, proj, ctxo, valo, grads, dk_acc, dv_acc,
    part, f_l, f_r, o_l, o_r, z_r, z_l, stage, total, ssem, rsem,
):
    f32, bf16 = jnp.float32, jnp.bfloat16
    y, zl, zh, x, c = where_am_i()
    me = zh * 8 + x * 2 + c
    left, right = (x + NX - 1) % NX, (x + 1) % NX
    opp = (x + 2) % NX
    to_left, to_right = device(y, zl, zh, left, c), device(y, zl, zh, right, c)
    to_core = device(y, zl, zh, x, 1 - c)
    to_far = device(y, zl, 1 - zh, x, c)
    y_lo, y_hi, y_op = (y + NY - 1) % NY, (y + 1) % NY, (y + 2) % NY
    to_ylo, to_yhi = device(y_lo, zl, zh, x, c), device(y_hi, zl, zh, x, c)
    has_lo, has_hi = zl > 0, zl < NL - 1
    to_zlo, to_zhi = device(y, zl - 1, zh, x, c), device(y, zl + 1, zh, x, c)

    def peer(d):
        return (y * NL + zl, (me + d) % 16)

    for d in range(1, 16):
        signal(peer(d))

    @pl.when(has_lo)
    def _():
        signal(to_zlo)

    @pl.when(has_hi)
    def _():
        signal(to_zhi)

    signal(to_ylo)
    signal(to_yhi)

    own = me * 64
    for q in range(NQ):
        t = tok[q * QR : (q + 1) * QR, :].astype(f32)
        mean_sq = jnp.mean(t * t, axis=1, keepdims=True)
        n = (t * lax.rsqrt(mean_sq + epsilon) * gain[...]).astype(bf16)
        nrm[pl.ds(pl.multiple_of(own + q * QR, QR), QR), :] = n
    w_all[pl.ds(pl.multiple_of((y * NL + zl) * BLK, 16), BLK), :] = w[...]

    ends = (zl == 0).astype(jnp.int32) + (zl == NL - 1).astype(jnp.int32)
    pl.semaphore_wait(pltpu.get_barrier_semaphore(), 19 - ends)

    sent = []
    used = [0]

    def send(src, dst, r, target):
        s = used[0]
        used[0] += 1
        copy = pltpu.make_async_remote_copy(
            src_ref=src, dst_ref=dst, send_sem=ssem.at[s], recv_sem=rsem.at[r],
            device_id=target, device_id_type=MESH,
        )
        copy.start()
        sent.append(copy)

    def got(ref, r):
        pltpu.make_async_remote_copy(
            src_ref=ref, dst_ref=ref, send_sem=ssem.at[0], recv_sem=rsem.at[r],
            device_id=to_core, device_id_type=MESH,
        ).wait_recv()

    def rows(h, xx, cc, q):
        r = h * 512 + xx * 128 + cc * 64 + q * QR
        return nrm.at[pl.ds(pl.multiple_of(r, QR), QR), :]

    def wrows(yy, b):
        return w_all.at[pl.ds(pl.multiple_of((yy * NL + b) * BLK, 16), BLK), :]

    def to_sister(k, h, xx, q):
        send(rows(h, xx, c, q), rows(h, xx, c, q), SEM.at["C"] + k * 16 + xx * 4 + q, to_core)

    def spread(k, h, q):
        mine = rows(h, x, c, q)
        send(mine, mine, SEM.at["L"] + k * 4 + q, to_right)
        send(mine, mine, SEM.at["R"] + k * 4 + q, to_left)
        to_sister(k, h, x, q)

    def relay(k, h, q):
        from_left, from_right = rows(h, left, c, q), rows(h, right, c, q)
        got(from_left, SEM.at["L"] + k * 4 + q)
        if q % 2 == 0:
            send(from_left, from_left, SEM.at["O"] + k * 4 + q, to_right)
        to_sister(k, h, left, q)
        got(from_right, SEM.at["R"] + k * 4 + q)
        if q % 2 == 1:
            send(from_right, from_right, SEM.at["O"] + k * 4 + q, to_left)
        to_sister(k, h, right, q)

    def last(k, h, q):
        got(rows(h, opp, c, q), SEM.at["O"] + k * 4 + q)
        to_sister(k, h, opp, q)

    line = []

    def along(cond, src, slot, r, target):
        def copy():
            return pltpu.make_async_remote_copy(
                src_ref=src, dst_ref=src, send_sem=ssem.at[N_SEND - 32 + slot],
                recv_sem=rsem.at[r], device_id=target, device_id_type=MESH,
            )

        @pl.when(cond)
        def _():
            copy().start()

        line.append((cond, copy))

    def y_copies(b):
        ref = wrows(y, b)
        for k, to, box in ((0, to_yhi, "YL"), (1, to_ylo, "YR")):
            yield pltpu.make_async_remote_copy(
                src_ref=ref, dst_ref=ref, send_sem=ssem.at[N_SEND - 48 + 8 * k + b],
                recv_sem=rsem.at[SEM.at[box] + b], device_id=to, device_id_type=MESH,
            )

    def y_spread(b):
        for copy in y_copies(b):
            copy.start()

    def w_step(t):
        lo_ok, hi_ok = zl - t >= 0, zl + t <= NL - 1
        b_lo, b_hi = jnp.maximum(zl - t, 0), jnp.minimum(zl + t, NL - 1)

        @pl.when(lo_ok)
        def _():
            got(wrows(y, b_lo), SEM.at["WR"] + t)

        if t < NL - 1:
            along(lo_ok & has_hi, wrows(y, b_lo), t, SEM.at["WR"] + t + 1, to_zhi)

        @pl.when(hi_ok)
        def _():
            got(wrows(y, b_hi), SEM.at["WL"] + t)

        if t < NL - 1:
            along(hi_ok & has_lo, wrows(y, b_hi), 8 + t, SEM.at["WL"] + t + 1, to_zlo)

        @pl.when(lo_ok)
        def _():
            y_spread(b_lo)

        @pl.when(hi_ok)
        def _():
            y_spread(b_hi)

    def y_relay(b):
        lo, hi = wrows(y_lo, b), wrows(y_hi, b)
        got(lo, SEM.at["YL"] + b)
        if b % 2 == 0:
            send(lo, lo, SEM.at["YO"] + b, to_yhi)
        got(hi, SEM.at["YR"] + b)
        if b % 2 == 1:
            send(hi, hi, SEM.at["YO"] + b, to_ylo)

    far = 1 - zh
    along(has_hi, wrows(y, zl), 0, SEM.at["WR"] + 1, to_zhi)
    along(has_lo, wrows(y, zl), 8, SEM.at["WL"] + 1, to_zlo)
    for q in range(NQ):
        spread(0, zh, q)
    y_spread(zl)

    def to_other_half(q):
        send(rows(zh, x, c, q), rows(zh, x, c, q), SEM.at["Z"] + q, to_far)

    here = pl.ds(pl.multiple_of(me * 64, 64), 64)
    mycols = pl.ds(pl.multiple_of(me * HD, HD), HD)
    slot = x * 2 + c

    def heads_to(d, h, k):
        t = h * 8 + (slot + d) % 8
        cols = pl.ds(pl.multiple_of(t * HD, HD), HD)
        to = (y * NL + zl, t)
        send(ctx.at[:, cols], ctxo.at[here, :], SEM.at["AC"] + k * 8 + d, to)
        send(val.at[:, cols], valo.at[here, :], SEM.at["AV"] + k * 8 + d, to)

    def heads_from(d, h, k):
        there = pl.ds(pl.multiple_of((h * 8 + (slot + 8 - d) % 8) * 64, 64), 64)
        got(ctxo.at[there, :], SEM.at["AC"] + k * 8 + d)
        got(valo.at[there, :], SEM.at["AV"] + k * 8 + d)

    for d in range(1, 8):
        heads_to(d, zh, 0)
    ctxo[here, :] = ctx[:, mycols]
    valo[here, :] = val[:, mycols]

    def sister(k, h):
        for xx in range(NX):
            for q in range(NQ):
                got(rows(h, xx, 1 - c, q), SEM.at["C"] + k * 16 + xx * 4 + q)

    def project(h):
        for r in range(2):
            p = pl.ds(pl.multiple_of(h * 512 + r * 256, 256), 256)
            proj[p, :] = jnp.dot(nrm[p, :], w_all[...], preferred_element_type=f32).astype(bf16)

    def from_far(q):
        got(rows(far, x, c, q), SEM.at["Z"] + q)
        spread(1, far, q)
        if q < 2:
            to_other_half(q + 2)
        elif q == 2:
            for d in range(8):
                heads_to(d, far, 1)
        if q > 0:
            relay(1, far, q - 1)
        if q > 1:
            last(1, far, q - 2)

    w_step(1)
    relay(0, zh, 0)
    w_step(2)
    w_step(3)
    relay(0, zh, 1)
    last(0, zh, 0)
    w_step(4)
    w_step(5)
    relay(0, zh, 2)
    last(0, zh, 1)
    w_step(6)
    to_other_half(0)
    to_other_half(1)
    w_step(7)
    relay(0, zh, 3)
    last(0, zh, 2)
    last(0, zh, 3)
    for b in range(4):
        y_relay(b)
    from_far(0)
    for b in range(4, 8):
        y_relay(b)
    from_far(1)
    for b in range(NL):
        got(wrows(y_op, b), SEM.at["YO"] + b)
    sister(0, zh)
    project(zh)
    from_far(2)
    from_far(3)
    relay(1, far, NQ - 1)
    last(1, far, NQ - 2)
    last(1, far, NQ - 1)
    sister(1, far)
    project(far)
    for d in range(8):
        if d > 0:
            heads_from(d, zh, 0)
        heads_from(d, far, 1)

    attention(proj, ctxo, valo, start, grads, dk_acc, dv_acc)

    def unit(n):
        i = lax.broadcasted_iota(jnp.int32, (n, n), 0)
        j = lax.broadcasted_iota(jnp.int32, (n, n), 1)
        return jnp.where(i == j, 1.0, 0.0).astype(bf16)

    nt = (((1,), (1,)), ((), ()))
    grads_t[...] = lax.dot_general(
        unit(3 * HD), grads[...], nt, preferred_element_type=f32
    ).astype(bf16)

    def compute(slot, yy):
        for j in range(0, WIDE, 384):
            cols = pl.ds(pl.multiple_of(yy * WIDE + j, 128), 384)
            p = jnp.dot(grads_t[...], nrm[:, cols], preferred_element_type=f32).astype(bf16)
            part[slot, j : j + 384, :] = lax.dot_general(
                unit(384), p, nt, preferred_element_type=f32
            ).astype(bf16)

    def blk(b):
        return slice(b * BLK, (b + 1) * BLK)

    def at(b):
        return pl.ds(pl.multiple_of(b * BLK, 16), BLK)

    compute(2, y_op)
    for m in range(4):
        src = 7 - m
        send(part.at[2, blk(src), :], f_l.at[blk(src), :], SEM.at["FL"] + src, to_yhi)
        send(part.at[2, blk(m), :], f_r.at[blk(m), :], SEM.at["FR"] + m, to_ylo)
    compute(1, y_hi)
    compute(3, y_lo)
    for m in range(4):
        b = 7 - m
        got(f_l.at[blk(b), :], SEM.at["FL"] + b)
        part[1, blk(b), :] = (part[1, blk(b), :].astype(f32) + f_l[blk(b), :].astype(f32)).astype(bf16)
        send(part.at[1, blk(b), :], o_l.at[blk(b), :], SEM.at["OL"] + b, to_yhi)
        send(part.at[3, blk(b), :], o_r.at[blk(b), :], SEM.at["OR"] + b, to_ylo)
        got(f_r.at[blk(m), :], SEM.at["FR"] + m)
        part[3, blk(m), :] = (part[3, blk(m), :].astype(f32) + f_r[blk(m), :].astype(f32)).astype(bf16)
        send(part.at[1, blk(m), :], o_l.at[blk(m), :], SEM.at["OL"] + m, to_yhi)
        send(part.at[3, blk(m), :], o_r.at[blk(m), :], SEM.at["OR"] + m, to_ylo)
    compute(0, y)

    s_line = N_SEND - 16

    def pass_on(cond, b, first, inbox, box_name, target, slot):
        def copy():
            return pltpu.make_async_remote_copy(
                src_ref=stage.at[at(b), :], dst_ref=inbox.at[at(b), :],
                send_sem=ssem.at[s_line + slot], recv_sem=rsem.at[SEM.at[box_name] + b],
                device_id=target, device_id_type=MESH,
            )

        @pl.when(cond)
        def _():
            @pl.when(jnp.logical_not(first))
            def _():
                got(inbox.at[at(b), :], SEM.at[box_name] + b)
                stage[at(b), :] = (total[at(b), :] + inbox[at(b), :].astype(f32)).astype(bf16)

            @pl.when(first)
            def _():
                stage[at(b), :] = total[at(b), :].astype(bf16)

            copy().start()

        line.append((cond, copy))

    for s in range(NL - 1):
        if s < 4:
            for b in (7 - s, s):
                got(o_l.at[blk(b), :], SEM.at["OL"] + b)
                got(o_r.at[blk(b), :], SEM.at["OR"] + b)
                total[blk(b), :] = (
                    part[0, blk(b), :].astype(f32)
                    + o_l[blk(b), :].astype(f32)
                    + o_r[blk(b), :].astype(f32)
                )
        b = jnp.minimum(NL - 1 + zl - s, NL - 1)
        pass_on(s >= zl, b, zl == 0, z_r, "ZR", to_zhi, s)
        b = jnp.maximum(s - (NL - 1) + zl, 0)
        pass_on(s >= NL - 1 - zl, b, zl == NL - 1, z_l, "ZL", to_zlo, 8 + s)

    @pl.when(has_lo)
    def _():
        got(z_r.at[at(zl), :], SEM.at["ZR"] + zl)
        total[at(zl), :] += z_r[at(zl), :].astype(f32)

    @pl.when(has_hi)
    def _():
        got(z_l.at[at(zl), :], SEM.at["ZL"] + zl)
        total[at(zl), :] += z_l[at(zl), :].astype(f32)

    for j in range(3):
        out[j] = total[at(zl), j * HD : (j + 1) * HD].astype(bf16)
    assert used[0] <= N_SEND - 48
    for copy in sent:
        copy.wait_send()
    for b in range(NL):
        for copy in y_copies(b):
            copy.wait_send()
    for cond, copy in line:

        @pl.when(cond)
        def _(copy=copy):
            copy().wait_send()


def local(tokens, gain, qk_weight, value_rows, context_grad, first_key):
    f32, bf16 = jnp.float32, jnp.bfloat16
    start = (first_key - lax.axis_index("dp") * SEQ).reshape(SEQ, 1)
    wide = pltpu.VMEM((WIDE, 3 * HD), bf16)
    out = pl.pallas_call(
        kernel,
        out_shape=jax.ShapeDtypeStruct((3, BLK, HD), bf16),
        in_specs=[VMEM] * 6,
        out_specs=VMEM,
        scratch_shapes=[
            pltpu.VMEM((SEQ, D), bf16),
            pltpu.VMEM((3 * HD, SEQ), bf16),
            pltpu.VMEM((D, 2 * HD), bf16),
            pltpu.VMEM((SEQ, 2 * HD), bf16),
            pltpu.VMEM((SEQ, HD), bf16),
            pltpu.VMEM((SEQ, HD), bf16),
            pltpu.VMEM((SEQ, 3 * HD), bf16),
            pltpu.VMEM((SEQ, HD), f32),
            pltpu.VMEM((SEQ, HD), f32),
            pltpu.VMEM((4, WIDE, 3 * HD), bf16),
            wide, wide, wide, wide, wide, wide, wide,
            pltpu.VMEM((WIDE, 3 * HD), f32),
            pltpu.SemaphoreType.DMA((N_SEND,)),
            pltpu.SemaphoreType.DMA((SEM.n,)),
        ],
        compiler_params=pltpu.CompilerParams(
            collective_id=0, has_side_effects=True, vmem_limit_bytes=58 << 20
        ),
        name="layer",
    )(tokens, gain.reshape(1, D), qk_weight.reshape(BLK, 2 * HD), context_grad, value_rows, start)
    return jnp.transpose(out, (1, 0, 2))


def solution(mesh):
    placed = (
        P(("dp", "tensor"), None),
        P(),
        P("dp", None, "tensor"),
        P(("dp", "tensor"), None),
        P(("dp", "tensor"), None),
        P("dp"),
    )
    return jax.shard_map(
        local, mesh=mesh, in_specs=placed, out_specs=P("dp", None, "tensor"), check_vma=False
    )
```

```python
import functools

import functools

import jax
import jax.numpy as jnp
from jax import lax
from jax.experimental import pallas as pl
from jax.experimental.pallas import tpu as pltpu
from jax.sharding import PartitionSpec as P

MESH = pl.DeviceIdType.MESH
HD = 128
epsilon = 1e-06
softcap = 50.0
query_scale = 144.0 ** (-0.5)
NX, NY, NL = 4, 4, 8
SEQ = 1024
D = 4608
BLK = 144
QR = 16
NQ = 4
VMEM = pl.BlockSpec(memory_space=pltpu.VMEM)


def where_am_i():
    dp, t = lax.axis_index("dp"), lax.axis_index("tensor")
    return dp // NL, dp % NL, t // 8, (t // 2) % NX, t % 2


def device(y, zl, zh, x, c):
    return (y * NL + zl, zh * 8 + x * 2 + c)


def signal(target):
    pl.semaphore_signal(
        pltpu.get_barrier_semaphore(), inc=1, device_id=target, device_id_type=MESH
    )


class Sems:
    def __init__(self):
        self.at = {}
        self.n = 0

    def block(self, name, count):
        self.at[name] = self.n
        self.n += count


SEM = Sems()
for name, count in (
    ("L", 8), ("R", 8), ("O", 8), ("C", 32), ("Z", 4), ("WR", 8), ("WL", 8),
    ("YL", 8), ("YR", 8), ("YO", 8), ("AC", 16), ("AV", 16),
    ("FL", 8), ("FR", 8), ("OL", 8), ("OR", 8), ("ZR", 24), ("ZL", 24),
):
    SEM.block(name, count)
N_SEND = 240
WIDE = D // NY


QB = 256
NT = (((1,), (1,)), ((), ()))
TN = (((0,), (0,)), ((), ()))


def softmax_part(proj, start, probs_t, slope_t):
    for lo in range(0, SEQ, QB):
        nk = lo + QB
        raw = lax.dot_general(
            proj[0:nk, HD : 2 * HD], proj[lo:nk, 0:HD], NT, preferred_element_type=jnp.float32
        )
        t = jnp.tanh(raw * (query_scale / softcap))
        keys = lax.broadcasted_iota(jnp.int32, (nk, QB), 0)
        pos = lo + lax.broadcasted_iota(jnp.int32, (nk, QB), 1)
        seen = (keys >= start[:, lo:nk]) & (keys <= pos)
        raised = jnp.where(seen, jnp.exp(t * softcap), 0.0)
        probs_t[0:nk, lo:nk] = raised * (1.0 / jnp.sum(raised, axis=0, keepdims=True))
        slope_t[0:nk, lo:nk] = (1.0 - t * t) * query_scale


def gradient_part(proj, ctx, val, probs_t, slope_t, grads_t, dk_acc, dv_acc):
    f32, bf16 = jnp.float32, jnp.bfloat16
    dk_acc[...] = jnp.zeros_like(dk_acc)
    dv_acc[...] = jnp.zeros_like(dv_acc)
    for lo in range(0, SEQ, QB):
        nk = lo + QB
        cot = ctx[lo:nk, :]
        probs = probs_t[0:nk, lo:nk]
        dv_acc[0:nk, :] += jnp.dot(probs.astype(bf16), cot, preferred_element_type=f32)
        dprobs = lax.dot_general(val[0:nk, :], cot, NT, preferred_element_type=f32)
        inner = jnp.sum(probs * dprobs, axis=0, keepdims=True)
        ds = (probs * (dprobs - inner) * slope_t[0:nk, lo:nk]).astype(bf16)
        grads_t[0:HD, lo:nk] = lax.dot_general(
            proj[0:nk, HD : 2 * HD], ds, TN, preferred_element_type=f32
        ).astype(bf16)
        dk_acc[0:nk, :] += jnp.dot(ds, proj[lo:nk, 0:HD], preferred_element_type=f32)
    for k, acc in ((1, dk_acc), (2, dv_acc)):
        grads_t[k * HD : (k + 1) * HD, :] = lax.dot_general(
            unit(HD), acc[...].astype(bf16), NT, preferred_element_type=f32
        ).astype(bf16)


def unit(n):
    i = lax.broadcasted_iota(jnp.int32, (n, n), 0)
    j = lax.broadcasted_iota(jnp.int32, (n, n), 1)
    return jnp.where(i == j, 1.0, 0.0).astype(jnp.bfloat16)


def kernel(
    tok, gain, w, ctx, val, start, out,
    nrm, grads_t, w_all, w_wide, proj, ctxo, valo, probs_t, slope_t, dk_acc, dv_acc,
    part, f_l, f_r, o_l, o_r, z_r, z_l, stage, total, ssem, rsem,
):
    f32, bf16 = jnp.float32, jnp.bfloat16
    y, zl, zh, x, c = where_am_i()
    me = zh * 8 + x * 2 + c
    left, right = (x + NX - 1) % NX, (x + 1) % NX
    opp = (x + 2) % NX
    to_left, to_right = device(y, zl, zh, left, c), device(y, zl, zh, right, c)
    to_core = device(y, zl, zh, x, 1 - c)
    to_far = device(y, zl, 1 - zh, x, c)
    y_lo, y_hi, y_op = (y + NY - 1) % NY, (y + 1) % NY, (y + 2) % NY
    to_ylo, to_yhi = device(y_lo, zl, zh, x, c), device(y_hi, zl, zh, x, c)
    has_lo, has_hi = zl > 0, zl < NL - 1
    to_zlo, to_zhi = device(y, zl - 1, zh, x, c), device(y, zl + 1, zh, x, c)

    def peer(d):
        return (y * NL + zl, (me + d) % 16)

    for d in range(1, 16):
        signal(peer(d))

    @pl.when(has_lo)
    def _():
        signal(to_zlo)

    @pl.when(has_hi)
    def _():
        signal(to_zhi)

    signal(to_ylo)
    signal(to_yhi)

    own = me * 64
    for q in range(NQ):
        t = tok[q * QR : (q + 1) * QR, :].astype(f32)
        mean_sq = jnp.mean(t * t, axis=1, keepdims=True)
        n = (t * lax.rsqrt(mean_sq + epsilon) * gain[...]).astype(bf16)
        nrm[pl.ds(pl.multiple_of(own + q * QR, QR), QR), :] = n
    w_wide[...] = w[...].astype(f32)
    for j in range(2):
        w_all[pl.ds(pl.multiple_of((y * NL + zl) * BLK, 16), BLK), j * HD : (j + 1) * HD] = w_wide[
            pl.ds(j, BLK, stride=2), :
        ].astype(bf16)

    ends = (zl == 0).astype(jnp.int32) + (zl == NL - 1).astype(jnp.int32)
    pl.semaphore_wait(pltpu.get_barrier_semaphore(), 19 - ends)

    sent = []
    used = [0]

    def send(src, dst, r, target):
        s = used[0]
        used[0] += 1
        copy = pltpu.make_async_remote_copy(
            src_ref=src, dst_ref=dst, send_sem=ssem.at[s], recv_sem=rsem.at[r],
            device_id=target, device_id_type=MESH,
        )
        copy.start()
        sent.append(copy)

    def got(ref, r):
        pltpu.make_async_remote_copy(
            src_ref=ref, dst_ref=ref, send_sem=ssem.at[0], recv_sem=rsem.at[r],
            device_id=to_core, device_id_type=MESH,
        ).wait_recv()

    def rows(h, xx, cc, q):
        r = h * 512 + xx * 128 + cc * 64 + q * QR
        return nrm.at[pl.ds(pl.multiple_of(r, QR), QR), :]

    def wrows(yy, b):
        return w_all.at[pl.ds(pl.multiple_of((yy * NL + b) * BLK, 16), BLK), :]

    def to_sister(k, h, xx, q):
        send(rows(h, xx, c, q), rows(h, xx, c, q), SEM.at["C"] + k * 16 + xx * 4 + q, to_core)

    def spread(k, h, q):
        mine = rows(h, x, c, q)
        send(mine, mine, SEM.at["L"] + k * 4 + q, to_right)
        send(mine, mine, SEM.at["R"] + k * 4 + q, to_left)
        to_sister(k, h, x, q)

    def relay(k, h, q):
        from_left, from_right = rows(h, left, c, q), rows(h, right, c, q)
        got(from_left, SEM.at["L"] + k * 4 + q)
        if q % 2 == 0:
            send(from_left, from_left, SEM.at["O"] + k * 4 + q, to_right)
        to_sister(k, h, left, q)
        got(from_right, SEM.at["R"] + k * 4 + q)
        if q % 2 == 1:
            send(from_right, from_right, SEM.at["O"] + k * 4 + q, to_left)
        to_sister(k, h, right, q)

    def last(k, h, q):
        got(rows(h, opp, c, q), SEM.at["O"] + k * 4 + q)
        to_sister(k, h, opp, q)

    line = []

    def along(cond, src, slot, r, target):
        def copy():
            return pltpu.make_async_remote_copy(
                src_ref=src, dst_ref=src, send_sem=ssem.at[N_SEND - 32 + slot],
                recv_sem=rsem.at[r], device_id=target, device_id_type=MESH,
            )

        @pl.when(cond)
        def _():
            copy().start()

        line.append((cond, copy))

    def y_copies(b):
        ref = wrows(y, b)
        for k, to, box in ((0, to_yhi, "YL"), (1, to_ylo, "YR")):
            yield pltpu.make_async_remote_copy(
                src_ref=ref, dst_ref=ref, send_sem=ssem.at[N_SEND - 48 + 8 * k + b],
                recv_sem=rsem.at[SEM.at[box] + b], device_id=to, device_id_type=MESH,
            )

    def y_spread(b):
        for copy in y_copies(b):
            copy.start()

    def w_step(t):
        lo_ok, hi_ok = zl - t >= 0, zl + t <= NL - 1
        b_lo, b_hi = jnp.maximum(zl - t, 0), jnp.minimum(zl + t, NL - 1)

        @pl.when(lo_ok)
        def _():
            got(wrows(y, b_lo), SEM.at["WR"] + t)

        if t < NL - 1:
            along(lo_ok & has_hi, wrows(y, b_lo), t, SEM.at["WR"] + t + 1, to_zhi)

        @pl.when(hi_ok)
        def _():
            got(wrows(y, b_hi), SEM.at["WL"] + t)

        if t < NL - 1:
            along(hi_ok & has_lo, wrows(y, b_hi), 8 + t, SEM.at["WL"] + t + 1, to_zlo)

        @pl.when(lo_ok)
        def _():
            y_spread(b_lo)

        @pl.when(hi_ok)
        def _():
            y_spread(b_hi)

    def y_relay(b):
        lo, hi = wrows(y_lo, b), wrows(y_hi, b)
        got(lo, SEM.at["YL"] + b)
        if b % 2 == 0:
            send(lo, lo, SEM.at["YO"] + b, to_yhi)
        got(hi, SEM.at["YR"] + b)
        if b % 2 == 1:
            send(hi, hi, SEM.at["YO"] + b, to_ylo)

    far = 1 - zh
    along(has_hi, wrows(y, zl), 0, SEM.at["WR"] + 1, to_zhi)
    along(has_lo, wrows(y, zl), 8, SEM.at["WL"] + 1, to_zlo)
    for q in range(NQ):
        spread(0, zh, q)
    y_spread(zl)
    send(rows(zh, x, c, 0), rows(zh, x, c, 0), SEM.at["Z"], to_far)

    def to_other_half(q):
        send(rows(zh, x, c, q), rows(zh, x, c, q), SEM.at["Z"] + q, to_far)

    here = pl.ds(pl.multiple_of(me * 64, 64), 64)
    mycols = pl.ds(pl.multiple_of(me * HD, HD), HD)
    slot = x * 2 + c

    def heads_to(d, h, k):
        t = h * 8 + (slot + d) % 8
        cols = pl.ds(pl.multiple_of(t * HD, HD), HD)
        to = (y * NL + zl, t)
        send(ctx.at[:, cols], ctxo.at[here, :], SEM.at["AC"] + k * 8 + d, to)
        send(val.at[:, cols], valo.at[here, :], SEM.at["AV"] + k * 8 + d, to)

    def heads_from(d, h, k):
        there = pl.ds(pl.multiple_of((h * 8 + (slot + 8 - d) % 8) * 64, 64), 64)
        got(ctxo.at[there, :], SEM.at["AC"] + k * 8 + d)
        got(valo.at[there, :], SEM.at["AV"] + k * 8 + d)

    for d in range(1, 8):
        heads_to(d, zh, 0)
    ctxo[here, :] = ctx[:, mycols]
    valo[here, :] = val[:, mycols]

    def sister(k, h):
        for xx in range(NX):
            for q in range(NQ):
                got(rows(h, xx, 1 - c, q), SEM.at["C"] + k * 16 + xx * 4 + q)

    def project(h):
        for r in range(2):
            p = pl.ds(pl.multiple_of(h * 512 + r * 256, 256), 256)
            proj[p, :] = jnp.dot(nrm[p, :], w_all[...], preferred_element_type=f32).astype(bf16)

    def from_far(q):
        got(rows(far, x, c, q), SEM.at["Z"] + q)
        spread(1, far, q)
        if q < 2:
            to_other_half(q + 2)
        elif q == 2:
            for d in range(8):
                heads_to(d, far, 1)
        if q > 0:
            relay(1, far, q - 1)
        if q > 1:
            last(1, far, q - 2)

    w_step(1)
    relay(0, zh, 0)
    w_step(2)
    w_step(3)
    relay(0, zh, 1)
    last(0, zh, 0)
    w_step(4)
    w_step(5)
    relay(0, zh, 2)
    last(0, zh, 1)
    w_step(6)
    to_other_half(1)
    w_step(7)
    relay(0, zh, 3)
    last(0, zh, 2)
    last(0, zh, 3)
    for b in range(4):
        y_relay(b)
    from_far(0)
    for b in range(4, 8):
        y_relay(b)
    from_far(1)
    for b in range(NL):
        got(wrows(y_op, b), SEM.at["YO"] + b)
    sister(0, zh)
    project(zh)
    from_far(2)
    from_far(3)
    relay(1, far, NQ - 1)
    last(1, far, NQ - 2)
    last(1, far, NQ - 1)
    sister(1, far)
    project(far)
    softmax_part(proj, start, probs_t, slope_t)
    for d in range(8):
        if d > 0:
            heads_from(d, zh, 0)
        heads_from(d, far, 1)

    gradient_part(proj, ctxo, valo, probs_t, slope_t, grads_t, dk_acc, dv_acc)

    def compute(slot, yy):
        for j in range(0, WIDE, 384):
            cols = pl.ds(pl.multiple_of(yy * WIDE + j, 128), 384)
            p = jnp.dot(grads_t[...], nrm[:, cols], preferred_element_type=f32).astype(bf16)
            part[slot, j : j + 384, :] = lax.dot_general(
                unit(384), p, NT, preferred_element_type=f32
            ).astype(bf16)

    def blk(b):
        return slice(b * BLK, (b + 1) * BLK)

    def at(b):
        return pl.ds(pl.multiple_of(b * BLK, 16), BLK)

    compute(2, y_op)
    for m in range(4):
        src = 7 - m
        send(part.at[2, blk(src), :], f_l.at[blk(src), :], SEM.at["FL"] + src, to_yhi)
        send(part.at[2, blk(m), :], f_r.at[blk(m), :], SEM.at["FR"] + m, to_ylo)
    compute(1, y_hi)
    compute(3, y_lo)
    for m in range(4):
        b = 7 - m
        got(f_l.at[blk(b), :], SEM.at["FL"] + b)
        part[1, blk(b), :] = (part[1, blk(b), :].astype(f32) + f_l[blk(b), :].astype(f32)).astype(bf16)
        send(part.at[1, blk(b), :], o_l.at[blk(b), :], SEM.at["OL"] + b, to_yhi)
        send(part.at[3, blk(b), :], o_r.at[blk(b), :], SEM.at["OR"] + b, to_ylo)
        got(f_r.at[blk(m), :], SEM.at["FR"] + m)
        part[3, blk(m), :] = (part[3, blk(m), :].astype(f32) + f_r[blk(m), :].astype(f32)).astype(bf16)
        send(part.at[1, blk(m), :], o_l.at[blk(m), :], SEM.at["OL"] + m, to_yhi)
        send(part.at[3, blk(m), :], o_r.at[blk(m), :], SEM.at["OR"] + m, to_ylo)
    compute(0, y)


    def pass_on(cond, b, first, inbox, box_name, target, slot):
        def copy(j):
            return pltpu.make_async_remote_copy(
                src_ref=stage.at[j, at(b), :], dst_ref=inbox.at[j, at(b), :],
                send_sem=ssem.at[N_SEND + slot * 3 + j],
                recv_sem=rsem.at[SEM.at[box_name] + 8 * j + b],
                device_id=target, device_id_type=MESH,
            )

        @pl.when(cond)
        def _():
            for j in range(3):

                @pl.when(jnp.logical_not(first))
                def _(j=j):
                    got(inbox.at[j, at(b), :], SEM.at[box_name] + 8 * j + b)
                    stage[j, at(b), :] = (
                        total[j, at(b), :] + inbox[j, at(b), :].astype(f32)
                    ).astype(bf16)

                @pl.when(first)
                def _(j=j):
                    stage[j, at(b), :] = total[j, at(b), :].astype(bf16)

                copy(j).start()

        for j in range(3):
            line.append((cond, functools.partial(copy, j)))

    for s in range(NL - 1):
        if s < 4:
            for b in (7 - s, s):
                got(o_l.at[blk(b), :], SEM.at["OL"] + b)
                got(o_r.at[blk(b), :], SEM.at["OR"] + b)
                for j in range(3):
                    c3 = slice(j * HD, (j + 1) * HD)
                    total[j, blk(b), :] = (
                        part[0, blk(b), c3].astype(f32)
                        + o_l[blk(b), c3].astype(f32)
                        + o_r[blk(b), c3].astype(f32)
                    )
        b = jnp.minimum(NL - 1 + zl - s, NL - 1)
        pass_on(s >= zl, b, zl == 0, z_r, "ZR", to_zhi, s)
        b = jnp.maximum(s - (NL - 1) + zl, 0)
        pass_on(s >= NL - 1 - zl, b, zl == NL - 1, z_l, "ZL", to_zlo, 8 + s)

    for j in range(3):

        @pl.when(has_lo)
        def _(j=j):
            got(z_r.at[j, at(zl), :], SEM.at["ZR"] + 8 * j + zl)
            total[j, at(zl), :] += z_r[j, at(zl), :].astype(f32)

        @pl.when(has_hi)
        def _(j=j):
            got(z_l.at[j, at(zl), :], SEM.at["ZL"] + 8 * j + zl)
            total[j, at(zl), :] += z_l[j, at(zl), :].astype(f32)

        out[j] = total[j, at(zl), :].astype(bf16)
    assert used[0] <= N_SEND - 48
    for copy in sent:
        copy.wait_send()
    for b in range(NL):
        for copy in y_copies(b):
            copy.wait_send()
    for cond, copy in line:

        @pl.when(cond)
        def _(copy=copy):
            copy().wait_send()


def local(tokens, gain, qk_weight, value_rows, context_grad, first_key):
    f32, bf16 = jnp.float32, jnp.bfloat16
    start = (first_key - lax.axis_index("dp") * SEQ).reshape(1, SEQ)
    wide, deep = pltpu.VMEM((WIDE, 3 * HD), bf16), pltpu.VMEM((3, WIDE, HD), bf16)
    out = pl.pallas_call(
        kernel,
        out_shape=jax.ShapeDtypeStruct((3, BLK, HD), bf16),
        in_specs=[VMEM] * 6,
        out_specs=VMEM,
        scratch_shapes=[
            pltpu.VMEM((SEQ, D), bf16),
            pltpu.VMEM((3 * HD, SEQ), bf16),
            pltpu.VMEM((D, 2 * HD), bf16),
            pltpu.VMEM((2 * BLK, HD), f32),
            pltpu.VMEM((SEQ, 2 * HD), bf16),
            pltpu.VMEM((SEQ, HD), bf16),
            pltpu.VMEM((SEQ, HD), bf16),
            pltpu.VMEM((SEQ, SEQ), f32),
            pltpu.VMEM((SEQ, SEQ), f32),
            pltpu.VMEM((SEQ, HD), f32),
            pltpu.VMEM((SEQ, HD), f32),
            pltpu.VMEM((4, WIDE, 3 * HD), bf16),
            wide, wide, wide, wide, deep, deep, deep,
            pltpu.VMEM((3, WIDE, HD), f32),
            pltpu.SemaphoreType.DMA((N_SEND + 48,)),
            pltpu.SemaphoreType.DMA((SEM.n,)),
        ],
        compiler_params=pltpu.CompilerParams(
            collective_id=0, has_side_effects=True, vmem_limit_bytes=58 << 20
        ),
        name="layer",
    )(tokens, gain.reshape(1, D), qk_weight.reshape(2 * BLK, HD), context_grad, value_rows, start)
    return jnp.transpose(out, (1, 0, 2))


def solution(mesh):
    placed = (
        P(("dp", "tensor"), None),
        P(),
        P("dp", None, "tensor"),
        P(("dp", "tensor"), None),
        P(("dp", "tensor"), None),
        P("dp"),
    )
    return jax.shard_map(
        local, mesh=mesh, in_specs=placed, out_specs=P("dp", None, "tensor"), check_vma=False
    )
```

```python
import functools

import functools

import jax
import jax.numpy as jnp
from jax import lax
from jax.experimental import pallas as pl
from jax.experimental.pallas import tpu as pltpu
from jax.sharding import PartitionSpec as P

MESH = pl.DeviceIdType.MESH
HD = 128
epsilon = 1e-06
softcap = 50.0
query_scale = 144.0 ** (-0.5)
NX, NY, NL = 4, 4, 8
SEQ = 1024
D = 4608
BLK = 144
QR = 16
NQ = 4
VMEM = pl.BlockSpec(memory_space=pltpu.VMEM)


def where_am_i():
    dp, t = lax.axis_index("dp"), lax.axis_index("tensor")
    return dp // NL, dp % NL, t // 8, (t // 2) % NX, t % 2


def device(y, zl, zh, x, c):
    return (y * NL + zl, zh * 8 + x * 2 + c)


def signal(target):
    pl.semaphore_signal(
        pltpu.get_barrier_semaphore(), inc=1, device_id=target, device_id_type=MESH
    )


class Sems:
    def __init__(self):
        self.at = {}
        self.n = 0

    def block(self, name, count):
        self.at[name] = self.n
        self.n += count


SEM = Sems()
for name, count in (
    ("L", 8), ("R", 8), ("O", 8), ("C", 32), ("Z", 4), ("WR", 8), ("WL", 8),
    ("YL", 8), ("YR", 8), ("YO", 8), ("AC", 16), ("AV", 16),
    ("FL", 8), ("FR", 8), ("OL", 8), ("OR", 8), ("ZR", 24), ("ZL", 24),
):
    SEM.block(name, count)
N_SEND = 240
WIDE = D // NY


QB = 256
NT = (((1,), (1,)), ((), ()))
TN = (((0,), (0,)), ((), ()))


def softmax_part(proj, start, probs_t, slope_t):
    for lo in range(0, SEQ, QB):
        nk = lo + QB
        raw = lax.dot_general(
            proj[0:nk, HD : 2 * HD], proj[lo:nk, 0:HD], NT, preferred_element_type=jnp.float32
        )
        t = jnp.tanh(raw * (query_scale / softcap))
        keys = lax.broadcasted_iota(jnp.int32, (nk, QB), 0)
        pos = lo + lax.broadcasted_iota(jnp.int32, (nk, QB), 1)
        seen = (keys >= start[:, lo:nk]) & (keys <= pos)
        raised = jnp.where(seen, jnp.exp(t * softcap), 0.0)
        probs_t[0:nk, lo:nk] = raised * (1.0 / jnp.sum(raised, axis=0, keepdims=True))
        slope_t[0:nk, lo:nk] = (1.0 - t * t) * query_scale


def gradient_part(proj, ctx, val, probs_t, slope_t, grads_t, dk_acc, dv_acc):
    f32, bf16 = jnp.float32, jnp.bfloat16
    dk_acc[...] = jnp.zeros_like(dk_acc)
    dv_acc[...] = jnp.zeros_like(dv_acc)
    for lo in range(0, SEQ, QB):
        nk = lo + QB
        cot = ctx[lo:nk, :]
        probs = probs_t[0:nk, lo:nk]
        dv_acc[0:nk, :] += jnp.dot(probs.astype(bf16), cot, preferred_element_type=f32)
        dprobs = lax.dot_general(val[0:nk, :], cot, NT, preferred_element_type=f32)
        inner = jnp.sum(probs * dprobs, axis=0, keepdims=True)
        ds = (probs * (dprobs - inner) * slope_t[0:nk, lo:nk]).astype(bf16)
        grads_t[0:HD, lo:nk] = lax.dot_general(
            proj[0:nk, HD : 2 * HD], ds, TN, preferred_element_type=f32
        ).astype(bf16)
        dk_acc[0:nk, :] += jnp.dot(ds, proj[lo:nk, 0:HD], preferred_element_type=f32)
    for k, acc in ((1, dk_acc), (2, dv_acc)):
        grads_t[k * HD : (k + 1) * HD, :] = lax.dot_general(
            unit(HD), acc[...].astype(bf16), NT, preferred_element_type=f32
        ).astype(bf16)


def unit(n):
    i = lax.broadcasted_iota(jnp.int32, (n, n), 0)
    j = lax.broadcasted_iota(jnp.int32, (n, n), 1)
    return jnp.where(i == j, 1.0, 0.0).astype(jnp.bfloat16)


def kernel(
    tok, gain, w, ctx, val, start, out,
    nrm, grads_t, w_all, w_wide, proj, ctxo, valo, probs_t, slope_t, dk_acc, dv_acc,
    part, f_l, f_r, o_l, o_r, z_r, z_l, stage, total, ssem, rsem,
):
    f32, bf16 = jnp.float32, jnp.bfloat16
    y, zl, zh, x, c = where_am_i()
    me = zh * 8 + x * 2 + c
    left, right = (x + NX - 1) % NX, (x + 1) % NX
    opp = (x + 2) % NX
    to_left, to_right = device(y, zl, zh, left, c), device(y, zl, zh, right, c)
    to_core = device(y, zl, zh, x, 1 - c)
    to_far = device(y, zl, 1 - zh, x, c)
    y_lo, y_hi, y_op = (y + NY - 1) % NY, (y + 1) % NY, (y + 2) % NY
    to_ylo, to_yhi = device(y_lo, zl, zh, x, c), device(y_hi, zl, zh, x, c)
    has_lo, has_hi = zl > 0, zl < NL - 1
    to_zlo, to_zhi = device(y, zl - 1, zh, x, c), device(y, zl + 1, zh, x, c)

    def peer(d):
        return (y * NL + zl, (me + d) % 16)

    for d in range(1, 16):
        signal(peer(d))

    @pl.when(has_lo)
    def _():
        signal(to_zlo)

    @pl.when(has_hi)
    def _():
        signal(to_zhi)

    signal(to_ylo)
    signal(to_yhi)

    own = me * 64
    for q in range(NQ):
        t = tok[q * QR : (q + 1) * QR, :].astype(f32)
        mean_sq = jnp.mean(t * t, axis=1, keepdims=True)
        n = (t * lax.rsqrt(mean_sq + epsilon) * gain[...]).astype(bf16)
        nrm[pl.ds(pl.multiple_of(own + q * QR, QR), QR), :] = n
    w_wide[...] = w[...].astype(f32)
    for j in range(2):
        w_all[pl.ds(pl.multiple_of((y * NL + zl) * BLK, 16), BLK), j * HD : (j + 1) * HD] = w_wide[
            pl.ds(j, BLK, stride=2), :
        ].astype(bf16)

    ends = (zl == 0).astype(jnp.int32) + (zl == NL - 1).astype(jnp.int32)
    pl.semaphore_wait(pltpu.get_barrier_semaphore(), 19 - ends)

    sent = []
    used = [0]

    def send(src, dst, r, target):
        s = used[0]
        used[0] += 1
        copy = pltpu.make_async_remote_copy(
            src_ref=src, dst_ref=dst, send_sem=ssem.at[s], recv_sem=rsem.at[r],
            device_id=target, device_id_type=MESH,
        )
        copy.start()
        sent.append(copy)

    def got(ref, r):
        pltpu.make_async_remote_copy(
            src_ref=ref, dst_ref=ref, send_sem=ssem.at[0], recv_sem=rsem.at[r],
            device_id=to_core, device_id_type=MESH,
        ).wait_recv()

    def rows(h, xx, cc, q):
        r = h * 512 + xx * 128 + cc * 64 + q * QR
        return nrm.at[pl.ds(pl.multiple_of(r, QR), QR), :]

    def wrows(yy, b):
        return w_all.at[pl.ds(pl.multiple_of((yy * NL + b) * BLK, 16), BLK), :]

    def to_sister(k, h, xx, q):
        send(rows(h, xx, c, q), rows(h, xx, c, q), SEM.at["C"] + k * 16 + xx * 4 + q, to_core)

    def spread(k, h, q):
        mine = rows(h, x, c, q)
        send(mine, mine, SEM.at["L"] + k * 4 + q, to_right)
        send(mine, mine, SEM.at["R"] + k * 4 + q, to_left)
        to_sister(k, h, x, q)

    def relay(k, h, q):
        from_left, from_right = rows(h, left, c, q), rows(h, right, c, q)
        got(from_left, SEM.at["L"] + k * 4 + q)
        if q % 2 == 0:
            send(from_left, from_left, SEM.at["O"] + k * 4 + q, to_right)
        to_sister(k, h, left, q)
        got(from_right, SEM.at["R"] + k * 4 + q)
        if q % 2 == 1:
            send(from_right, from_right, SEM.at["O"] + k * 4 + q, to_left)
        to_sister(k, h, right, q)

    def last(k, h, q):
        got(rows(h, opp, c, q), SEM.at["O"] + k * 4 + q)
        to_sister(k, h, opp, q)

    line = []

    def along(cond, src, slot, r, target):
        def copy():
            return pltpu.make_async_remote_copy(
                src_ref=src, dst_ref=src, send_sem=ssem.at[N_SEND - 32 + slot],
                recv_sem=rsem.at[r], device_id=target, device_id_type=MESH,
            )

        @pl.when(cond)
        def _():
            copy().start()

        line.append((cond, copy))

    def y_copies(b):
        ref = wrows(y, b)
        for k, to, box in ((0, to_yhi, "YL"), (1, to_ylo, "YR")):
            yield pltpu.make_async_remote_copy(
                src_ref=ref, dst_ref=ref, send_sem=ssem.at[N_SEND - 48 + 8 * k + b],
                recv_sem=rsem.at[SEM.at[box] + b], device_id=to, device_id_type=MESH,
            )

    def y_spread(b):
        for copy in y_copies(b):
            copy.start()

    def w_step(t):
        lo_ok, hi_ok = zl - t >= 0, zl + t <= NL - 1
        b_lo, b_hi = jnp.maximum(zl - t, 0), jnp.minimum(zl + t, NL - 1)

        @pl.when(lo_ok)
        def _():
            got(wrows(y, b_lo), SEM.at["WR"] + t)

        if t < NL - 1:
            along(lo_ok & has_hi, wrows(y, b_lo), t, SEM.at["WR"] + t + 1, to_zhi)

        @pl.when(hi_ok)
        def _():
            got(wrows(y, b_hi), SEM.at["WL"] + t)

        if t < NL - 1:
            along(hi_ok & has_lo, wrows(y, b_hi), 8 + t, SEM.at["WL"] + t + 1, to_zlo)

        @pl.when(lo_ok)
        def _():
            y_spread(b_lo)

        @pl.when(hi_ok)
        def _():
            y_spread(b_hi)

    def y_relay(b):
        lo, hi = wrows(y_lo, b), wrows(y_hi, b)
        got(lo, SEM.at["YL"] + b)
        if b % 2 == 0:
            send(lo, lo, SEM.at["YO"] + b, to_yhi)
        got(hi, SEM.at["YR"] + b)
        if b % 2 == 1:
            send(hi, hi, SEM.at["YO"] + b, to_ylo)

    far = 1 - zh
    along(has_hi, wrows(y, zl), 0, SEM.at["WR"] + 1, to_zhi)
    along(has_lo, wrows(y, zl), 8, SEM.at["WL"] + 1, to_zlo)
    for q in range(NQ):
        spread(0, zh, q)
    y_spread(zl)
    send(rows(zh, x, c, 0), rows(zh, x, c, 0), SEM.at["Z"], to_far)

    def to_other_half(q):
        send(rows(zh, x, c, q), rows(zh, x, c, q), SEM.at["Z"] + q, to_far)

    here = pl.ds(pl.multiple_of(me * 64, 64), 64)
    mycols = pl.ds(pl.multiple_of(me * HD, HD), HD)
    slot = x * 2 + c

    def heads_to(d, h, k):
        t = h * 8 + (slot + d) % 8
        cols = pl.ds(pl.multiple_of(t * HD, HD), HD)
        to = (y * NL + zl, t)
        send(ctx.at[:, cols], ctxo.at[here, :], SEM.at["AC"] + k * 8 + d, to)
        send(val.at[:, cols], valo.at[here, :], SEM.at["AV"] + k * 8 + d, to)

    def heads_from(d, h, k):
        there = pl.ds(pl.multiple_of((h * 8 + (slot + 8 - d) % 8) * 64, 64), 64)
        got(ctxo.at[there, :], SEM.at["AC"] + k * 8 + d)
        got(valo.at[there, :], SEM.at["AV"] + k * 8 + d)

    for d in range(1, 8):
        heads_to(d, zh, 0)
    ctxo[here, :] = ctx[:, mycols]
    valo[here, :] = val[:, mycols]

    def sister(k, h):
        for xx in range(NX):
            for q in range(NQ):
                got(rows(h, xx, 1 - c, q), SEM.at["C"] + k * 16 + xx * 4 + q)

    def project(h):
        for r in range(2):
            p = pl.ds(pl.multiple_of(h * 512 + r * 256, 256), 256)
            proj[p, :] = jnp.dot(nrm[p, :], w_all[...], preferred_element_type=f32).astype(bf16)

    def from_far(q):
        got(rows(far, x, c, q), SEM.at["Z"] + q)
        spread(1, far, q)
        if q == 1:
            for d in range(8):
                heads_to(d, far, 1)
        if q > 0:
            relay(1, far, q - 1)
        if q > 1:
            last(1, far, q - 2)

    w_step(1)
    relay(0, zh, 0)
    w_step(2)
    w_step(3)
    relay(0, zh, 1)
    last(0, zh, 0)
    w_step(4)
    w_step(5)
    relay(0, zh, 2)
    last(0, zh, 1)
    w_step(6)
    to_other_half(1)
    to_other_half(2)
    to_other_half(3)
    w_step(7)
    relay(0, zh, 3)
    last(0, zh, 2)
    last(0, zh, 3)
    for b in range(4):
        y_relay(b)
    from_far(0)
    for b in range(4, 8):
        y_relay(b)
    from_far(1)
    for b in range(NL):
        got(wrows(y_op, b), SEM.at["YO"] + b)
    sister(0, zh)
    project(zh)
    from_far(2)
    from_far(3)
    relay(1, far, NQ - 1)
    last(1, far, NQ - 2)
    last(1, far, NQ - 1)
    sister(1, far)
    project(far)
    softmax_part(proj, start, probs_t, slope_t)
    for d in range(8):
        if d > 0:
            heads_from(d, zh, 0)
        heads_from(d, far, 1)

    gradient_part(proj, ctxo, valo, probs_t, slope_t, grads_t, dk_acc, dv_acc)

    def compute(slot, yy):
        for j in range(0, WIDE, 384):
            cols = pl.ds(pl.multiple_of(yy * WIDE + j, 128), 384)
            p = jnp.dot(grads_t[...], nrm[:, cols], preferred_element_type=f32).astype(bf16)
            part[slot, j : j + 384, :] = lax.dot_general(
                unit(384), p, NT, preferred_element_type=f32
            ).astype(bf16)

    def blk(b):
        return slice(b * BLK, (b + 1) * BLK)

    def at(b):
        return pl.ds(pl.multiple_of(b * BLK, 16), BLK)

    compute(2, y_op)
    for m in range(4):
        src = 7 - m
        send(part.at[2, blk(src), :], f_l.at[blk(src), :], SEM.at["FL"] + src, to_yhi)
        send(part.at[2, blk(m), :], f_r.at[blk(m), :], SEM.at["FR"] + m, to_ylo)
    compute(1, y_hi)
    compute(3, y_lo)
    for m in range(4):
        b = 7 - m
        got(f_l.at[blk(b), :], SEM.at["FL"] + b)
        part[1, blk(b), :] = (part[1, blk(b), :].astype(f32) + f_l[blk(b), :].astype(f32)).astype(bf16)
        send(part.at[1, blk(b), :], o_l.at[blk(b), :], SEM.at["OL"] + b, to_yhi)
        send(part.at[3, blk(b), :], o_r.at[blk(b), :], SEM.at["OR"] + b, to_ylo)
        got(f_r.at[blk(m), :], SEM.at["FR"] + m)
        part[3, blk(m), :] = (part[3, blk(m), :].astype(f32) + f_r[blk(m), :].astype(f32)).astype(bf16)
        send(part.at[1, blk(m), :], o_l.at[blk(m), :], SEM.at["OL"] + m, to_yhi)
        send(part.at[3, blk(m), :], o_r.at[blk(m), :], SEM.at["OR"] + m, to_ylo)
    compute(0, y)


    def pass_on(cond, b, first, inbox, box_name, target, slot):
        def copy(j):
            return pltpu.make_async_remote_copy(
                src_ref=stage.at[j, at(b), :], dst_ref=inbox.at[j, at(b), :],
                send_sem=ssem.at[N_SEND + slot * 3 + j],
                recv_sem=rsem.at[SEM.at[box_name] + 8 * j + b],
                device_id=target, device_id_type=MESH,
            )

        @pl.when(cond)
        def _():
            for j in range(3):

                @pl.when(jnp.logical_not(first))
                def _(j=j):
                    got(inbox.at[j, at(b), :], SEM.at[box_name] + 8 * j + b)
                    stage[j, at(b), :] = (
                        total[j, at(b), :] + inbox[j, at(b), :].astype(f32)
                    ).astype(bf16)

                @pl.when(first)
                def _(j=j):
                    stage[j, at(b), :] = total[j, at(b), :].astype(bf16)

                copy(j).start()

        for j in range(3):
            line.append((cond, functools.partial(copy, j)))

    for s in range(NL - 1):
        if s < 4:
            for b in (7 - s, s):
                got(o_l.at[blk(b), :], SEM.at["OL"] + b)
                got(o_r.at[blk(b), :], SEM.at["OR"] + b)
                for j in range(3):
                    c3 = slice(j * HD, (j + 1) * HD)
                    total[j, blk(b), :] = (
                        part[0, blk(b), c3].astype(f32)
                        + o_l[blk(b), c3].astype(f32)
                        + o_r[blk(b), c3].astype(f32)
                    )
        b = jnp.minimum(NL - 1 + zl - s, NL - 1)
        pass_on(s >= zl, b, zl == 0, z_r, "ZR", to_zhi, s)
        b = jnp.maximum(s - (NL - 1) + zl, 0)
        pass_on(s >= NL - 1 - zl, b, zl == NL - 1, z_l, "ZL", to_zlo, 8 + s)

    for j in range(3):

        @pl.when(has_lo)
        def _(j=j):
            got(z_r.at[j, at(zl), :], SEM.at["ZR"] + 8 * j + zl)
            total[j, at(zl), :] += z_r[j, at(zl), :].astype(f32)

        @pl.when(has_hi)
        def _(j=j):
            got(z_l.at[j, at(zl), :], SEM.at["ZL"] + 8 * j + zl)
            total[j, at(zl), :] += z_l[j, at(zl), :].astype(f32)

        out[j] = total[j, at(zl), :].astype(bf16)
    assert used[0] <= N_SEND - 48
    for copy in sent:
        copy.wait_send()
    for b in range(NL):
        for copy in y_copies(b):
            copy.wait_send()
    for cond, copy in line:

        @pl.when(cond)
        def _(copy=copy):
            copy().wait_send()


def local(tokens, gain, qk_weight, value_rows, context_grad, first_key):
    f32, bf16 = jnp.float32, jnp.bfloat16
    start = (first_key - lax.axis_index("dp") * SEQ).reshape(1, SEQ)
    wide, deep = pltpu.VMEM((WIDE, 3 * HD), bf16), pltpu.VMEM((3, WIDE, HD), bf16)
    out = pl.pallas_call(
        kernel,
        out_shape=jax.ShapeDtypeStruct((3, BLK, HD), bf16),
        in_specs=[VMEM] * 6,
        out_specs=VMEM,
        scratch_shapes=[
            pltpu.VMEM((SEQ, D), bf16),
            pltpu.VMEM((3 * HD, SEQ), bf16),
            pltpu.VMEM((D, 2 * HD), bf16),
            pltpu.VMEM((2 * BLK, HD), f32),
            pltpu.VMEM((SEQ, 2 * HD), bf16),
            pltpu.VMEM((SEQ, HD), bf16),
            pltpu.VMEM((SEQ, HD), bf16),
            pltpu.VMEM((SEQ, SEQ), f32),
            pltpu.VMEM((SEQ, SEQ), f32),
            pltpu.VMEM((SEQ, HD), f32),
            pltpu.VMEM((SEQ, HD), f32),
            pltpu.VMEM((4, WIDE, 3 * HD), bf16),
            wide, wide, wide, wide, deep, deep, deep,
            pltpu.VMEM((3, WIDE, HD), f32),
            pltpu.SemaphoreType.DMA((N_SEND + 48,)),
            pltpu.SemaphoreType.DMA((SEM.n,)),
        ],
        compiler_params=pltpu.CompilerParams(
            collective_id=0, has_side_effects=True, vmem_limit_bytes=58 << 20
        ),
        name="layer",
    )(tokens, gain.reshape(1, D), qk_weight.reshape(2 * BLK, HD), context_grad, value_rows, start)
    return jnp.transpose(out, (1, 0, 2))


def solution(mesh):
    placed = (
        P(("dp", "tensor"), None),
        P(),
        P("dp", None, "tensor"),
        P(("dp", "tensor"), None),
        P(("dp", "tensor"), None),
        P("dp"),
    )
    return jax.shard_map(
        local, mesh=mesh, in_specs=placed, out_specs=P("dp", None, "tensor"), check_vma=False
    )
```
